32 devices in a mesh: grp: 2 (over y), ex: 4 (over z), layer: 4 (over x, core).
Axes of the slice: x: 2, y: 2, z: 4, core: 2. Of those that a mesh axis runs over, the one named last changes fastest.
Arguments:
- row_grads: bfloat16 [8, 16384, 1024], P('layer', ('grp', 'ex')), parts along dimension 1, may hold values from -0.1875 to 0.1875
- query_grads: bfloat16 [8, 256, 1024], P('layer', 'ex'), may hold values from -6 to 6
- fisher_inv: bfloat16 [8, 1024, 1024], P('layer'), as said below
Outputs:
- scores: float32 [16384, 256], P(('grp', 'ex'), 'layer'), parts along dimension 0
The draws below stay inside these ranges and needn't reach their ends.
There are 2 independent parts, one for each index of `grp`. The reference program is written for one: setup_inputs(seed, part) draws one part's arguments, and reference() takes and returns one part's arrays. A program takes and returns all parts, laid end to end along the dimension named above; an argument that names none is the same for every part. Nothing has to cross between parts.
Inputs may be any that keep to these rules, and one draw needn't show every extreme that they name: `fisher_inv`: each layer's matrix is a positive multiple of one with diagonal entries near 2 and independent off-diagonal entries.
All inputs are finite; a program needn't handle non-finite values.
Results may differ from the reference program's by a relative error of at most 0.0029.
Values may be sent and summed in bfloat16 or wider, within the bound.
A program may use at most 128 MiB of HBM per device.

```python
import jax
import jax.numpy as jnp
from jax import lax

PROJ = 1024
LAYERS = 8
ROWS = 8192
QUERIES = 256


def draw_fisher_inv(key, part):
    key = jax.random.fold_in(key, 7)
    noise_key, scale_key = jax.random.split(key)
    noise = jax.random.normal(noise_key, (LAYERS, PROJ, PROJ), jnp.float32)
    noise = noise * (0.5 / PROJ ** 0.5)
    layer_scale = jnp.exp(jax.random.uniform(scale_key, (LAYERS, 1, 1), jnp.float32, -0.7, 0.7))
    eye_part = jnp.eye(PROJ, dtype=jnp.float32) * 2.0
    return ((eye_part + noise) * layer_scale).astype(jnp.bfloat16)


def shard_levels(rng, shape, cuts, smallest, high):
    def one(dim, parts):
        steps = jax.random.uniform(jax.random.fold_in(jax.random.fold_in(rng, 6), dim), (parts,), jnp.float32, smallest / len(cuts), high / len(cuts))
        return jnp.repeat(jnp.exp(steps), shape[dim] // parts).reshape((-1,) + (1,) * (len(shape) - dim - 1))

    level = one(*cuts[0])
    for cut in cuts[1:]:
        level = level * one(*cut)
    return level


def centred(stream_key, extent, scale, limit, pieces=(), held_as=jnp.bfloat16):
    array = scale * jax.random.normal(stream_key, extent, jnp.float32)
    if pieces:
        array = array * shard_levels(stream_key, extent, pieces, -0.22, 0.18)
    return jnp.clip(array, -limit, limit).astype(held_as)


def setup_inputs(seed: int = 0, part: int = 0) -> dict:
    keys = jax.random.split(jax.random.key(seed), 4)
    part_splits = jax.random.split(jax.random.fold_in(keys[3], part), 4)
    return {
        "row_grads": centred(part_splits[0], (LAYERS, ROWS, PROJ), PROJ ** -0.5, 0.1875, ((0, 4), (1, 4))),
        "query_grads": centred(keys[1], (LAYERS, QUERIES, PROJ), 1.0, 6.0, ((0, 4), (1, 4))),
        "fisher_inv": draw_fisher_inv(jax.random.fold_in(keys[3], 71), part),
    }


def reference(row_grads, query_grads, fisher_inv):
    def one_layer(total, items):
        rows, queries, matrix = items
        prepared = jnp.dot(queries, matrix.T, preferred_element_type=jnp.float32).astype(jnp.bfloat16)
        return total + jnp.dot(rows, prepared.T, preferred_element_type=jnp.float32), None

    start = jnp.zeros((row_grads.shape[1], query_grads.shape[1]), jnp.float32)
    total, _ = lax.scan(one_layer, start, (row_grads, query_grads, fisher_inv))
    return total
```

```python
import functools

import jax
import jax.numpy as jnp
from jax import lax
from jax.experimental import pallas as pl
from jax.experimental.pallas import tpu as pltpu
from jax.sharding import PartitionSpec as P

MESH = pl.DeviceIdType.MESH
CHUNKS = 4


def precondition(queries, fisher_inv):
    return jnp.einsum(
        "lqk,ljk->lqj", queries, fisher_inv, preferred_element_type=jnp.float32
    ).astype(jnp.bfloat16)


def plain(row_grads, query_grads, fisher_inv):
    prepared_own = precondition(query_grads, fisher_inv)
    partial_scores = jnp.einsum(
        "lrp,lqp->rq",
        row_grads,
        lax.all_gather(prepared_own, "ex", axis=1, tiled=True),
        preferred_element_type=jnp.float32,
    )
    return lax.psum_scatter(partial_scores, "layer", scatter_dimension=1, tiled=True)


def dot_nt(a, b):
    return lax.dot_general(a, b, (((1,), (1,)), ((), ())), preferred_element_type=jnp.float32)


def kernel(rows_hbm, q_hbm, f_hbm, out_ref,
           rows, q, fisher, prep, keep, send_a, recv_a, send_b, recv_b,
           load_sem, row_sem, z_send, z_recv, y_send, y_recv, a_send, a_recv, b_send, b_recv):
    y = lax.axis_index("grp")
    z = lax.axis_index("ex")
    i = lax.axis_index("layer")
    x = i // 2
    c = i - 2 * x
    other_core = 2 * x + 1 - c
    other_x = 2 * (1 - x) + c
    total = rows.shape[1]
    step = total // CHUNKS

    loads = [pltpu.make_async_copy(q_hbm, q, load_sem.at[2])]
    loads += [pltpu.make_async_copy(f_hbm.at[y], fisher.at[0], load_sem.at[0])]
    loads += [pltpu.make_async_copy(f_hbm.at[1 - y], fisher.at[1], load_sem.at[1])]
    for copy in loads:
        copy.start()

    def row_copy(n):
        part = pl.ds(n * step, step)
        return pltpu.make_async_copy(rows_hbm.at[:, part], rows.at[:, part], row_sem.at[n])

    for n in range(CHUNKS):
        row_copy(n).start()

    barrier = pltpu.get_barrier_semaphore()
    for d in (1, 2, 3):
        pl.semaphore_signal(barrier, inc=1, device_id={"ex": (z + d) % 4}, device_id_type=MESH)
    pl.semaphore_signal(barrier, inc=1, device_id={"grp": 1 - y}, device_id_type=MESH)
    pl.semaphore_signal(barrier, inc=1, device_id={"layer": other_core}, device_id_type=MESH)
    pl.semaphore_signal(barrier, inc=1, device_id={"layer": other_x}, device_id_type=MESH)

    side = z // 2
    w = z + side * (3 - 2 * z)
    order = [o + side * (3 - 2 * o) for o in (w, 1 - w, 2, 3)]

    def z_copy(k):
        return pltpu.make_async_remote_copy(
            src_ref=prep.at[z, y], dst_ref=prep.at[z, y],
            send_sem=z_send.at[order[k]], recv_sem=z_recv.at[z],
            device_id={"ex": order[k]}, device_id_type=MESH)

    def z_arrival(k):
        s = order[k]
        return pltpu.make_async_remote_copy(
            src_ref=prep.at[s, y], dst_ref=prep.at[s, y],
            send_sem=z_send.at[s], recv_sem=z_recv.at[s],
            device_id={"ex": s}, device_id_type=MESH)

    def y_copy(k, layer):
        s = order[k]
        return pltpu.make_async_remote_copy(
            src_ref=prep.at[s, layer], dst_ref=prep.at[s, layer],
            send_sem=y_send.at[s], recv_sem=y_recv.at[s],
            device_id={"grp": 1 - y}, device_id_type=MESH)

    loads[0].wait()
    loads[1].wait()
    prep[z, y] = dot_nt(q[y], fisher[0]).astype(jnp.bfloat16)
    pl.semaphore_wait(barrier, 6)
    for k in (1, 2, 3):
        z_copy(k).start()
    loads[2].wait()
    prep[z, 1 - y] = dot_nt(q[1 - y], fisher[1]).astype(jnp.bfloat16)

    def a_copy(xi, n):
        part = pl.ds(pl.multiple_of(n * step, step), step)
        return pltpu.make_async_remote_copy(
            src_ref=send_a.at[xi, :, part], dst_ref=recv_a.at[xi, :, part],
            send_sem=a_send.at[xi, n], recv_sem=a_recv.at[xi, n],
            device_id={"layer": other_core}, device_id_type=MESH)

    def b_copy(n):
        part = pl.ds(pl.multiple_of(n * step, step), step)
        return pltpu.make_async_remote_copy(
            src_ref=send_b.at[:, part], dst_ref=recv_b.at[:, part],
            send_sem=b_send.at[n], recv_sem=b_recv.at[n],
            device_id={"layer": other_x}, device_id_type=MESH)

    def compute(k):
        s = order[k]
        xi = s // 2
        ci = s - 2 * xi

        @pl.loop(0, CHUNKS)
        def _(n):
            if k == 0:
                row_copy(n).wait()
            part = pl.ds(pl.multiple_of(n * step, step), step)
            value = dot_nt(prep[s, 0], rows[0, part]) + dot_nt(prep[s, 1], rows[1, part])

            @pl.when(ci == c)
            def _():
                keep[xi, :, part] = value

            @pl.when(ci != c)
            def _():
                send_a[xi, :, part] = value.astype(jnp.bfloat16)
                a_copy(xi, n).start()

    def reduce(k):
        s = order[k]
        xi = s // 2
        ci = s - 2 * xi

        @pl.when(ci == c)
        def _():
            @pl.loop(0, CHUNKS)
            def _(n):
                part = pl.ds(pl.multiple_of(n * step, step), step)
                a_copy(xi, n).wait_recv()
                value = keep[xi, :, part] + recv_a[xi, :, part].astype(jnp.float32)

                @pl.when(xi == x)
                def _():
                    out_ref[:, part] = value

                @pl.when(xi != x)
                def _():
                    send_b[:, part] = value.astype(jnp.bfloat16)
                    b_copy(n).start()

    def pass_on(k):
        z_arrival(k).wait_recv()
        y_copy(k, y).start()

    compute(0)
    pass_on(1)
    reduce(0)
    pass_on(2)
    y_copy(1, 1 - y).wait_recv()
    compute(1)
    pass_on(3)
    reduce(1)
    y_copy(2, 1 - y).wait_recv()
    compute(2)
    reduce(2)
    y_copy(3, 1 - y).wait_recv()
    compute(3)
    reduce(3)

    @pl.loop(0, CHUNKS)
    def _(n):
        part = pl.ds(pl.multiple_of(n * step, step), step)
        b_copy(n).wait_recv()
        out_ref[:, part] += recv_b[:, part].astype(jnp.float32)

    for k in (1, 2, 3):
        z_copy(k).wait_send()
        y_copy(k, y).wait_send()

    @pl.loop(0, CHUNKS)
    def _(n):
        a_copy(0, n).wait_send()
        a_copy(1, n).wait_send()
        b_copy(n).wait_send()


def fused(row_grads, query_grads, fisher_inv):
    layers, total, depth = row_grads.shape
    queries = query_grads.shape[1]
    bf16 = jnp.bfloat16
    dma = pltpu.SemaphoreType.DMA
    out = pl.pallas_call(
        kernel,
        out_shape=jax.ShapeDtypeStruct((queries, total), jnp.float32),
        in_specs=[pl.BlockSpec(memory_space=pl.ANY)] * 3,
        out_specs=pl.BlockSpec(memory_space=pltpu.VMEM),
        scratch_shapes=[
            pltpu.VMEM((layers, total, depth), bf16),
            pltpu.VMEM((layers, queries, depth), bf16),
            pltpu.VMEM((layers, depth, depth), bf16),
            pltpu.VMEM((4, layers, queries, depth), bf16),
            pltpu.VMEM((2, queries, total), jnp.float32),
            pltpu.VMEM((2, queries, total), bf16),
            pltpu.VMEM((2, queries, total), bf16),
            pltpu.VMEM((queries, total), bf16),
            pltpu.VMEM((queries, total), bf16),
            dma((3,)), dma((CHUNKS,)),
            dma((4,)), dma((4,)), dma((4,)), dma((4,)),
            dma((2, CHUNKS)), dma((2, CHUNKS)), dma((CHUNKS,)), dma((CHUNKS,)),
        ],
        compiler_params=pltpu.CompilerParams(
            collective_id=0, has_side_effects=True, vmem_limit_bytes=40 * 2**20
        ),
    )(row_grads, query_grads, fisher_inv)
    return out.T


def solution(mesh):
    in_specs = (P("layer", ("grp", "ex"), None), P("layer", "ex", None), P("layer", None, None))
    out_specs = P(("grp", "ex"), "layer")

    def run(row_grads, query_grads, fisher_inv):
        two_layers = row_grads.shape[0] == 8
        small = (mesh.shape["grp"], mesh.shape["ex"], mesh.shape["layer"]) == (2, 4, 4)
        local = fused if small and two_layers else plain
        return jax.shard_map(
            local, mesh=mesh, in_specs=in_specs, out_specs=out_specs, check_vma=False
        )(row_grads, query_grads, fisher_inv)

    return run
```

```python
import functools

import jax
import jax.numpy as jnp
from jax import lax
from jax.experimental import pallas as pl
from jax.experimental.pallas import tpu as pltpu
from jax.sharding import PartitionSpec as P

MESH = pl.DeviceIdType.MESH
CHUNKS = 4
HALVES = 2


def precondition(queries, fisher_inv):
    return jnp.einsum(
        "lqk,ljk->lqj", queries, fisher_inv, preferred_element_type=jnp.float32
    ).astype(jnp.bfloat16)


def plain(row_grads, query_grads, fisher_inv):
    prepared_own = precondition(query_grads, fisher_inv)
    partial_scores = jnp.einsum(
        "lrp,lqp->rq",
        row_grads,
        lax.all_gather(prepared_own, "ex", axis=1, tiled=True),
        preferred_element_type=jnp.float32,
    )
    return lax.psum_scatter(partial_scores, "layer", scatter_dimension=1, tiled=True)


def dot_nt(a, b):
    return lax.dot_general(a, b, (((1,), (1,)), ((), ())), preferred_element_type=jnp.float32)


def kernel(rows_hbm, q_hbm, f_hbm, out_ref,
           rows, q, fisher, prep, acc, keep, send_a, recv_a, send_b, recv_b,
           load_sem, row_sem, z_send, z_recv, y_send, y_recv, a_send, a_recv, b_send, b_recv):
    y = lax.axis_index("grp")
    z = lax.axis_index("ex")
    i = lax.axis_index("layer")
    x = i // 2
    c = i - 2 * x
    other_core = 2 * x + 1 - c
    other_x = 2 * (1 - x) + c
    total = rows.shape[1]
    step = total // CHUNKS
    half = q.shape[1] // HALVES

    side = z // 2
    w = z + side * (3 - 2 * z)
    mid = w == 1
    order = [o + side * (3 - 2 * o) for o in (w, 1 - w, 2, 3)]

    loads = [pltpu.make_async_copy(q_hbm, q, load_sem.at[2])]
    loads += [pltpu.make_async_copy(f_hbm.at[y], fisher.at[0], load_sem.at[0])]
    loads += [pltpu.make_async_copy(f_hbm.at[1 - y], fisher.at[1], load_sem.at[1])]
    for copy in loads:
        copy.start()

    def row_copy(n):
        part = pl.ds(n * step, step)
        return pltpu.make_async_copy(rows_hbm.at[:, part], rows.at[:, part], row_sem.at[n])

    barrier = pltpu.get_barrier_semaphore()

    def greet(**device):
        pl.semaphore_signal(barrier, inc=1, device_id=device, device_id_type=MESH)

    greet(ex=order[1])

    @pl.when(mid)
    def _():
        greet(ex=order[2])

    greet(grp=1 - y)
    greet(layer=other_core)
    greet(layer=other_x)

    def z_copy(shard, to, slot, h):
        part = pl.ds(h * half, half)
        return pltpu.make_async_remote_copy(
            src_ref=prep.at[shard, y, part], dst_ref=prep.at[shard, y, part],
            send_sem=z_send.at[slot, h], recv_sem=z_recv.at[shard, h],
            device_id={"ex": to}, device_id_type=MESH)

    def y_copy(k, layer, h):
        s = order[k]
        part = pl.ds(h * half, half)
        return pltpu.make_async_remote_copy(
            src_ref=prep.at[s, layer, part], dst_ref=prep.at[s, layer, part],
            send_sem=y_send.at[k, h], recv_sem=y_recv.at[k, h],
            device_id={"grp": 1 - y}, device_id_type=MESH)

    onward = {1: order[2], 2: order[1], 3: order[1]}

    def pass_on(k):
        for h in range(HALVES):
            z_copy(order[k], order[1], 1 + k, h).wait_recv()

            @pl.when(mid)
            def _():
                z_copy(order[k], onward[k], 1 + k, h).start()

            y_copy(k, y, h).start()

    loads[0].wait()
    loads[1].wait()
    for n in range(CHUNKS):
        row_copy(n).start()
    prep[z, y] = dot_nt(q[y], fisher[0]).astype(jnp.bfloat16)
    pl.semaphore_wait(barrier, 4 + w)
    for h in range(HALVES):
        z_copy(z, order[1], 0, h).start()

        @pl.when(mid)
        def _():
            z_copy(z, order[2], 1, h).start()

    loads[2].wait()
    prep[z, 1 - y] = dot_nt(q[1 - y], fisher[1]).astype(jnp.bfloat16)

    def a_copy(xi, n):
        part = pl.ds(pl.multiple_of(n * step, step), step)
        return pltpu.make_async_remote_copy(
            src_ref=send_a.at[xi, :, part], dst_ref=recv_a.at[xi, :, part],
            send_sem=a_send.at[xi, n], recv_sem=a_recv.at[xi, n],
            device_id={"layer": other_core}, device_id_type=MESH)

    def b_copy(n):
        part = pl.ds(pl.multiple_of(n * step, step), step)
        return pltpu.make_async_remote_copy(
            src_ref=send_b.at[:, part], dst_ref=recv_b.at[:, part],
            send_sem=b_send.at[n], recv_sem=b_recv.at[n],
            device_id={"layer": other_x}, device_id_type=MESH)

    def first(k):
        @pl.loop(0, CHUNKS)
        def _(n):
            part = pl.ds(pl.multiple_of(n * step, step), step)
            acc[k - 1, :, part] = dot_nt(prep[order[k], y], rows[y, part])

    def second(k):
        s = order[k]
        xi = s // 2
        ci = s - 2 * xi

        @pl.loop(0, CHUNKS)
        def _(n):
            part = pl.ds(pl.multiple_of(n * step, step), step)
            if k == 0:
                row_copy(n).wait()
                value = dot_nt(prep[s, 0], rows[0, part]) + dot_nt(prep[s, 1], rows[1, part])
            else:
                value = acc[k - 1, :, part] + dot_nt(prep[s, 1 - y], rows[1 - y, part])

            @pl.when(ci == c)
            def _():
                keep[xi, :, part] = value

            @pl.when(ci != c)
            def _():
                send_a[xi, :, part] = value.astype(jnp.bfloat16)
                a_copy(xi, n).start()

    def swapped(k):
        for h in range(HALVES):
            y_copy(k, 1 - y, h).wait_recv()

    def reduce(k):
        s = order[k]
        xi = s // 2
        ci = s - 2 * xi

        @pl.when(ci == c)
        def _():
            @pl.loop(0, CHUNKS)
            def _(n):
                part = pl.ds(pl.multiple_of(n * step, step), step)
                a_copy(xi, n).wait_recv()
                value = keep[xi, :, part] + recv_a[xi, :, part].astype(jnp.float32)

                @pl.when(xi == x)
                def _():
                    out_ref[:, part] = value

                @pl.when(xi != x)
                def _():
                    send_b[:, part] = value.astype(jnp.bfloat16)
                    b_copy(n).start()

    second(0)
    pass_on(1)

    @pl.when(mid)
    def _():
        pass_on(2)

    reduce(0)
    first(1)

    @pl.when(mid)
    def _():
        pass_on(3)

    @pl.when(jnp.logical_not(mid))
    def _():
        pass_on(2)

    first(2)
    swapped(1)
    second(1)

    @pl.when(jnp.logical_not(mid))
    def _():
        pass_on(3)

    first(3)
    reduce(1)
    swapped(2)
    second(2)
    reduce(2)
    swapped(3)
    second(3)
    reduce(3)

    @pl.loop(0, CHUNKS)
    def _(n):
        part = pl.ds(pl.multiple_of(n * step, step), step)
        b_copy(n).wait_recv()
        out_ref[:, part] += recv_b[:, part].astype(jnp.float32)

    for h in range(HALVES):
        z_copy(z, order[1], 0, h).wait_send()
        for k in (1, 2, 3):
            y_copy(k, y, h).wait_send()

        @pl.when(mid)
        def _():
            z_copy(z, order[2], 1, h).wait_send()
            for k in (1, 2, 3):
                z_copy(order[k], onward[k], 1 + k, h).wait_send()

    @pl.loop(0, CHUNKS)
    def _(n):
        a_copy(0, n).wait_send()
        a_copy(1, n).wait_send()
        b_copy(n).wait_send()


def fused(row_grads, query_grads, fisher_inv):
    layers, total, depth = row_grads.shape
    queries = query_grads.shape[1]
    bf16 = jnp.bfloat16
    dma = pltpu.SemaphoreType.DMA
    out = pl.pallas_call(
        kernel,
        out_shape=jax.ShapeDtypeStruct((queries, total), jnp.float32),
        in_specs=[pl.BlockSpec(memory_space=pl.ANY)] * 3,
        out_specs=pl.BlockSpec(memory_space=pltpu.VMEM),
        scratch_shapes=[
            pltpu.VMEM((layers, total, depth), bf16),
            pltpu.VMEM((layers, queries, depth), bf16),
            pltpu.VMEM((layers, depth, depth), bf16),
            pltpu.VMEM((4, layers, queries, depth), bf16),
            pltpu.VMEM((3, queries, total), jnp.float32),
            pltpu.VMEM((2, queries, total), jnp.float32),
            pltpu.VMEM((2, queries, total), bf16),
            pltpu.VMEM((2, queries, total), bf16),
            pltpu.VMEM((queries, total), bf16),
            pltpu.VMEM((queries, total), bf16),
            dma((3,)), dma((CHUNKS,)),
            dma((5, HALVES)), dma((4, HALVES)), dma((4, HALVES)), dma((4, HALVES)),
            dma((2, CHUNKS)), dma((2, CHUNKS)), dma((CHUNKS,)), dma((CHUNKS,)),
        ],
        compiler_params=pltpu.CompilerParams(
            collective_id=0, has_side_effects=True, vmem_limit_bytes=60 * 2**20
        ),
    )(row_grads, query_grads, fisher_inv)
    return out.T


def solution(mesh):
    in_specs = (P("layer", ("grp", "ex"), None), P("layer", "ex", None), P("layer", None, None))
    out_specs = P(("grp", "ex"), "layer")

    def run(row_grads, query_grads, fisher_inv):
        two_layers = row_grads.shape[0] == 8
        small = (mesh.shape["grp"], mesh.shape["ex"], mesh.shape["layer"]) == (2, 4, 4)
        local = fused if small and two_layers else plain
        return jax.shard_map(
            local, mesh=mesh, in_specs=in_specs, out_specs=out_specs, check_vma=False
        )(row_grads, query_grads, fisher_inv)

    return run
```

```python
import functools

import jax
import jax.numpy as jnp
from jax import lax
from jax.experimental import pallas as pl
from jax.experimental.pallas import tpu as pltpu
from jax.sharding import PartitionSpec as P

MESH = pl.DeviceIdType.MESH
CHUNKS = 2
LAST_CHUNKS = 2
HALVES = 2


def precondition(queries, fisher_inv):
    return jnp.einsum(
        "lqk,ljk->lqj", queries, fisher_inv, preferred_element_type=jnp.float32
    ).astype(jnp.bfloat16)


def plain(row_grads, query_grads, fisher_inv):
    prepared_own = precondition(query_grads, fisher_inv)
    partial_scores = jnp.einsum(
        "lrp,lqp->rq",
        row_grads,
        lax.all_gather(prepared_own, "ex", axis=1, tiled=True),
        preferred_element_type=jnp.float32,
    )
    return lax.psum_scatter(partial_scores, "layer", scatter_dimension=1, tiled=True)


def dot_nt(a, b):
    return lax.dot_general(a, b, (((1,), (1,)), ((), ())), preferred_element_type=jnp.float32)


def kernel(rows_hbm, q_hbm, f_hbm, out_ref,
           rows, q, fisher, prep, acc, keep, send_a, recv_a, send_b, recv_b,
           load_sem, row_sem, z_send, z_recv, y_send, y_recv, a_send, a_recv, b_send, b_recv):
    y = lax.axis_index("grp")
    z = lax.axis_index("ex")
    i = lax.axis_index("layer")
    x = i // 2
    c = i - 2 * x
    other_core = 2 * x + 1 - c
    other_x = 2 * (1 - x) + c
    total = rows.shape[1]
    step = total // CHUNKS
    half = q.shape[1] // HALVES

    side = z // 2
    w = z + side * (3 - 2 * z)
    mid = w == 1
    order = [o + side * (3 - 2 * o) for o in (w, 1 - w, 2, 3)]

    loads = [pltpu.make_async_copy(q_hbm, q, load_sem.at[2])]
    loads += [pltpu.make_async_copy(f_hbm.at[y], fisher.at[0], load_sem.at[0])]
    loads += [pltpu.make_async_copy(f_hbm.at[1 - y], fisher.at[1], load_sem.at[1])]
    for copy in loads:
        copy.start()

    def row_copy(n):
        part = pl.ds(n * step, step)
        return pltpu.make_async_copy(rows_hbm.at[:, part], rows.at[:, part], row_sem.at[n])

    barrier = pltpu.get_barrier_semaphore()

    def greet(**device):
        pl.semaphore_signal(barrier, inc=1, device_id=device, device_id_type=MESH)

    greet(ex=order[1])

    @pl.when(mid)
    def _():
        greet(ex=order[2])

    greet(grp=1 - y)
    greet(layer=other_core)
    greet(layer=other_x)

    def z_copy(shard, to, slot, h):
        part = pl.ds(h * half, half)
        return pltpu.make_async_remote_copy(
            src_ref=prep.at[shard, y, part], dst_ref=prep.at[shard, y, part],
            send_sem=z_send.at[slot, h], recv_sem=z_recv.at[shard, h],
            device_id={"ex": to}, device_id_type=MESH)

    def y_copy(k, layer, h):
        s = order[k]
        part = pl.ds(h * half, half)
        return pltpu.make_async_remote_copy(
            src_ref=prep.at[s, layer, part], dst_ref=prep.at[s, layer, part],
            send_sem=y_send.at[k, h], recv_sem=y_recv.at[k, h],
            device_id={"grp": 1 - y}, device_id_type=MESH)

    onward = {1: order[2], 2: order[1], 3: order[1]}

    def pass_on(k):
        for h in range(HALVES):
            z_copy(order[k], order[1], 1 + k, h).wait_recv()

            @pl.when(mid)
            def _():
                z_copy(order[k], onward[k], 1 + k, h).start()

            y_copy(k, y, h).start()

    loads[0].wait()
    loads[1].wait()
    for n in range(CHUNKS):
        row_copy(n).start()
    prep[z, y] = dot_nt(q[y], fisher[0]).astype(jnp.bfloat16)
    pl.semaphore_wait(barrier, 4 + w)
    for h in range(HALVES):
        z_copy(z, order[1], 0, h).start()

        @pl.when(mid)
        def _():
            z_copy(z, order[2], 1, h).start()

    loads[2].wait()
    prep[z, 1 - y] = dot_nt(q[1 - y], fisher[1]).astype(jnp.bfloat16)

    def tile(k, h, r):
        if k < 3:
            queries, chunks = pl.ds(0, half * HALVES), CHUNKS
        else:
            queries, chunks = pl.ds(h * half, half), LAST_CHUNKS
        size = total // chunks
        return queries, pl.ds(pl.multiple_of(r * size, size), size), h * chunks + r

    def place(k):
        s = order[k]
        return s, s // 2, s - 2 * (s // 2)

    def a_copy(k, h, r):
        xi = place(k)[1]
        queries, part, n = tile(k, h, r)
        return pltpu.make_async_remote_copy(
            src_ref=send_a.at[xi, queries, part], dst_ref=recv_a.at[xi, queries, part],
            send_sem=a_send.at[xi, n], recv_sem=a_recv.at[xi, n],
            device_id={"layer": other_core}, device_id_type=MESH)

    def b_copy(k, h, r):
        queries, part, n = tile(k, h, r)
        return pltpu.make_async_remote_copy(
            src_ref=send_b.at[queries, part], dst_ref=recv_b.at[queries, part],
            send_sem=b_send.at[n], recv_sem=b_recv.at[n],
            device_id={"layer": other_x}, device_id_type=MESH)

    def first(k):
        @pl.loop(0, CHUNKS)
        def _(r):
            part = pl.ds(pl.multiple_of(r * step, step), step)
            acc[k - 1, :, part] = dot_nt(prep[order[k], y], rows[y, part])

    def second(k, h, r):
        s, xi, ci = place(k)
        queries, part, _ = tile(k, h, r)
        if k == 0:
            row_copy(r).wait()
            value = dot_nt(prep[s, 0], rows[0, part]) + dot_nt(prep[s, 1], rows[1, part])
        else:
            value = acc[k - 1, queries, part] + dot_nt(prep[s, 1 - y, queries], rows[1 - y, part])

        @pl.when(ci == c)
        def _():
            keep[xi, queries, part] = value

        @pl.when(ci != c)
        def _():
            send_a[xi, queries, part] = value.astype(jnp.bfloat16)
            a_copy(k, h, r).start()

    def reduce(k, h, r):
        s, xi, ci = place(k)
        queries, part, _ = tile(k, h, r)

        @pl.when(ci == c)
        def _():
            a_copy(k, h, r).wait_recv()
            value = keep[xi, queries, part] + recv_a[xi, queries, part].astype(jnp.float32)

            @pl.when(xi == x)
            def _():
                out_ref[queries, part] = value

            @pl.when(xi != x)
            def _():
                send_b[queries, part] = value.astype(jnp.bfloat16)
                b_copy(k, h, r).start()

    def each(k, *steps):
        @pl.loop(0, CHUNKS if k < 3 else LAST_CHUNKS)
        def _(r):
            for work, h in steps:
                work(k, h, r)

    def swapped(k, h):
        y_copy(k, 1 - y, h).wait_recv()

    each(0, (second, 0))
    pass_on(1)

    @pl.when(mid)
    def _():
        pass_on(2)

    each(0, (reduce, 0))
    first(1)

    @pl.when(mid)
    def _():
        pass_on(3)

    @pl.when(jnp.logical_not(mid))
    def _():
        pass_on(2)

    first(2)
    for h in range(HALVES):
        swapped(1, h)
    each(1, (second, 0))

    @pl.when(jnp.logical_not(mid))
    def _():
        pass_on(3)

    first(3)
    each(1, (reduce, 0))
    for h in range(HALVES):
        swapped(2, h)
    each(2, (second, 0))
    each(2, (reduce, 0))
    for h in range(HALVES):
        swapped(3, h)
        each(3, (second, h), *([(reduce, h - 1)] if h else []))
    each(3, (reduce, HALVES - 1))

    def finish(k, h, r):
        queries, part, _ = tile(k, h, r)
        b_copy(k, h, r).wait_recv()
        out_ref[queries, part] += recv_b[queries, part].astype(jnp.float32)

    def a_sent(k, h, r):
        a_copy(k, h, r).wait_send()

    def b_sent(k, h, r):
        b_copy(k, h, r).wait_send()

    for k in range(4):
        s, xi, ci = place(k)
        parts = range(HALVES if k == 3 else 1)

        @pl.when(s == i)
        def _():
            for h in parts:
                each(k, (finish, h))

        @pl.when(ci != c)
        def _():
            for h in parts:
                each(k, (a_sent, h))

        @pl.when(s == other_x)
        def _():
            for h in parts:
                each(k, (b_sent, h))

    for h in range(HALVES):
        z_copy(z, order[1], 0, h).wait_send()
        for k in (1, 2, 3):
            y_copy(k, y, h).wait_send()

        @pl.when(mid)
        def _():
            z_copy(z, order[2], 1, h).wait_send()
            for k in (1, 2, 3):
                z_copy(order[k], onward[k], 1 + k, h).wait_send()


def fused(row_grads, query_grads, fisher_inv):
    layers, total, depth = row_grads.shape
    queries = query_grads.shape[1]
    bf16 = jnp.bfloat16
    dma = pltpu.SemaphoreType.DMA
    tiles = max(CHUNKS, HALVES * LAST_CHUNKS)
    out = pl.pallas_call(
        kernel,
        out_shape=jax.ShapeDtypeStruct((queries, total), jnp.float32),
        in_specs=[pl.BlockSpec(memory_space=pltpu.HBM)] * 3,
        out_specs=pl.BlockSpec(memory_space=pltpu.VMEM),
        scratch_shapes=[
            pltpu.VMEM((layers, total, depth), bf16),
            pltpu.VMEM((layers, queries, depth), bf16),
            pltpu.VMEM((layers, depth, depth), bf16),
            pltpu.VMEM((4, layers, queries, depth), bf16),
            pltpu.VMEM((3, queries, total), jnp.float32),
            pltpu.VMEM((2, queries, total), jnp.float32),
            pltpu.VMEM((2, queries, total), bf16),
            pltpu.VMEM((2, queries, total), bf16),
            pltpu.VMEM((queries, total), bf16),
            pltpu.VMEM((queries, total), bf16),
            dma((3,)), dma((CHUNKS,)),
            dma((5, HALVES)), dma((4, HALVES)), dma((4, HALVES)), dma((4, HALVES)),
            dma((2, tiles)), dma((2, tiles)), dma((tiles,)), dma((tiles,)),
        ],
        compiler_params=pltpu.CompilerParams(
            collective_id=0, has_side_effects=True, vmem_limit_bytes=50 * 2**20
        ),
    )(row_grads, query_grads, fisher_inv)
    return out.T


def solution(mesh):
    in_specs = (P("layer", ("grp", "ex"), None), P("layer", "ex", None), P("layer", None, None))
    out_specs = P(("grp", "ex"), "layer")

    def run(row_grads, query_grads, fisher_inv):
        two_layers = row_grads.shape[0] == 8
        small = (mesh.shape["grp"], mesh.shape["ex"], mesh.shape["layer"]) == (2, 4, 4)
        local = fused if small and two_layers else plain
        return jax.shard_map(
            local, mesh=mesh, in_specs=in_specs, out_specs=out_specs, check_vma=False
        )(row_grads, query_grads, fisher_inv)

    return run
```

```python
import functools

import jax
import jax.numpy as jnp
from jax import lax
from jax.experimental import pallas as pl
from jax.experimental.pallas import tpu as pltpu
from jax.sharding import PartitionSpec as P

MESH = pl.DeviceIdType.MESH
CHUNKS = 2
LAST_CHUNKS = 2
HALVES = 2


def precondition(queries, fisher_inv):
    return jnp.einsum(
        "lqk,ljk->lqj", queries, fisher_inv, preferred_element_type=jnp.float32
    ).astype(jnp.bfloat16)


def plain(row_grads, query_grads, fisher_inv):
    prepared_own = precondition(query_grads, fisher_inv)
    partial_scores = jnp.einsum(
        "lrp,lqp->rq",
        row_grads,
        lax.all_gather(prepared_own, "ex", axis=1, tiled=True),
        preferred_element_type=jnp.float32,
    )
    return lax.psum_scatter(partial_scores, "layer", scatter_dimension=1, tiled=True)


def dot_nt(a, b):
    return lax.dot_general(a, b, (((1,), (1,)), ((), ())), preferred_element_type=jnp.float32)


def kernel(rows_hbm, q_hbm, f_hbm, out_ref,
           rows, q, fisher, prep, acc, keep, send_a, recv_a, send_b, recv_b,
           load_sem, row_sem, z_send, z_recv, y_send, y_recv, a_send, a_recv, b_send, b_recv):
    y = lax.axis_index("grp")
    z = lax.axis_index("ex")
    i = lax.axis_index("layer")
    x = i // 2
    c = i - 2 * x
    other_core = 2 * x + 1 - c
    other_x = 2 * (1 - x) + c
    total = rows.shape[1]
    step = total // CHUNKS
    half = q.shape[1] // HALVES

    side = z // 2
    w = z + side * (3 - 2 * z)
    mid = w == 1
    order = [o + side * (3 - 2 * o) for o in (w, 1 - w, 2, 3)]

    loads = [pltpu.make_async_copy(q_hbm, q, load_sem.at[2])]
    loads += [pltpu.make_async_copy(f_hbm.at[y], fisher.at[0], load_sem.at[0])]
    loads += [pltpu.make_async_copy(f_hbm.at[1 - y], fisher.at[1], load_sem.at[1])]
    for copy in loads:
        copy.start()

    def row_copy(n):
        part = pl.ds(n * step, step)
        return pltpu.make_async_copy(rows_hbm.at[:, part], rows.at[:, part], row_sem.at[n])

    for n in range(CHUNKS):
        row_copy(n).start()

    barrier = pltpu.get_barrier_semaphore()

    def greet(**device):
        pl.semaphore_signal(barrier, inc=1, device_id=device, device_id_type=MESH)

    greet(ex=order[1])

    @pl.when(mid)
    def _():
        greet(ex=order[2])

    greet(grp=1 - y)
    greet(layer=other_core)
    greet(layer=other_x)

    def z_copy(shard, to, slot, h):
        part = pl.ds(h * half, half)
        return pltpu.make_async_remote_copy(
            src_ref=prep.at[shard, y, part], dst_ref=prep.at[shard, y, part],
            send_sem=z_send.at[slot, h], recv_sem=z_recv.at[shard, h],
            device_id={"ex": to}, device_id_type=MESH)

    def y_copy(k, layer, h):
        s = order[k]
        part = pl.ds(h * half, half)
        return pltpu.make_async_remote_copy(
            src_ref=prep.at[s, layer, part], dst_ref=prep.at[s, layer, part],
            send_sem=y_send.at[k, h], recv_sem=y_recv.at[k, h],
            device_id={"grp": 1 - y}, device_id_type=MESH)

    onward = {1: order[2], 2: order[1], 3: order[1]}

    def z_half(k, h):
        z_copy(order[k], order[1], 1 + k, h).wait_recv()

        @pl.when(mid)
        def _():
            z_copy(order[k], onward[k], 1 + k, h).start()

        y_copy(k, y, h).start()

    def pass_on(k):
        for h in range(HALVES):
            z_half(k, h)

    loads[0].wait()
    loads[1].wait()
    prep[z, y] = dot_nt(q[y], fisher[0]).astype(jnp.bfloat16)
    pl.semaphore_wait(barrier, 4 + w)
    for h in range(HALVES):
        z_copy(z, order[1], 0, h).start()

        @pl.when(mid)
        def _():
            z_copy(z, order[2], 1, h).start()

    loads[2].wait()
    prep[z, 1 - y] = dot_nt(q[1 - y], fisher[1]).astype(jnp.bfloat16)

    def tile(k, h, r):
        if k < 3:
            queries, chunks = pl.ds(0, half * HALVES), CHUNKS
        else:
            queries, chunks = pl.ds(h * half, half), LAST_CHUNKS
        size = total // chunks
        return queries, pl.ds(pl.multiple_of(r * size, size), size), h * chunks + r

    def place(k):
        s = order[k]
        return s, s // 2, s - 2 * (s // 2)

    def a_copy(k, h, r):
        xi = place(k)[1]
        queries, part, n = tile(k, h, r)
        return pltpu.make_async_remote_copy(
            src_ref=send_a.at[xi, queries, part], dst_ref=recv_a.at[xi, queries, part],
            send_sem=a_send.at[xi, n], recv_sem=a_recv.at[xi, n],
            device_id={"layer": other_core}, device_id_type=MESH)

    def b_copy(k, h, r):
        queries, part, n = tile(k, h, r)
        return pltpu.make_async_remote_copy(
            src_ref=send_b.at[queries, part], dst_ref=recv_b.at[queries, part],
            send_sem=b_send.at[n], recv_sem=b_recv.at[n],
            device_id={"layer": other_x}, device_id_type=MESH)

    def first(k):
        @pl.loop(0, CHUNKS)
        def _(r):
            part = pl.ds(pl.multiple_of(r * step, step), step)
            acc[k - 1, :, part] = dot_nt(prep[order[k], y], rows[y, part])

    def second(k, h, r):
        s, xi, ci = place(k)
        queries, part, _ = tile(k, h, r)
        if k == 0:
            row_copy(r).wait()
            value = dot_nt(prep[s, 0], rows[0, part]) + dot_nt(prep[s, 1], rows[1, part])
        else:
            value = acc[k - 1, queries, part] + dot_nt(prep[s, 1 - y, queries], rows[1 - y, part])

        @pl.when(ci == c)
        def _():
            keep[xi, queries, part] = value

        @pl.when(ci != c)
        def _():
            send_a[xi, queries, part] = value.astype(jnp.bfloat16)
            a_copy(k, h, r).start()

    def reduce(k, h, r):
        s, xi, ci = place(k)
        queries, part, _ = tile(k, h, r)

        @pl.when(ci == c)
        def _():
            a_copy(k, h, r).wait_recv()
            value = keep[xi, queries, part] + recv_a[xi, queries, part].astype(jnp.float32)

            @pl.when(xi == x)
            def _():
                out_ref[queries, part] = value

            @pl.when(xi != x)
            def _():
                send_b[queries, part] = value.astype(jnp.bfloat16)
                b_copy(k, h, r).start()

    def each(k, *steps):
        @pl.loop(0, CHUNKS if k < 3 else LAST_CHUNKS)
        def _(r):
            for work, h in steps:
                work(k, h, r)

    def swapped(k, h):
        y_copy(k, 1 - y, h).wait_recv()

    each(0, (second, 0))
    pass_on(1)

    @pl.when(mid)
    def _():
        pass_on(2)

    first(1)

    @pl.when(mid)
    def _():
        pass_on(3)

    @pl.when(jnp.logical_not(mid))
    def _():
        pass_on(2)

    first(2)
    each(0, (reduce, 0))
    for h in range(HALVES):
        swapped(1, h)
    second(1, 0, 0)

    @pl.when(jnp.logical_not(mid))
    def _():
        z_half(3, 0)

    for n in range(1, CHUNKS):
        second(1, 0, n)

    @pl.when(jnp.logical_not(mid))
    def _():
        for n in range(1, HALVES):
            z_half(3, n)

    first(3)
    each(1, (reduce, 0))
    for h in range(HALVES):
        swapped(2, h)
    each(2, (second, 0))
    each(2, (reduce, 0))
    for h in range(HALVES):
        swapped(3, h)
        each(3, (second, h), *([(reduce, h - 1)] if h else []))
    each(3, (reduce, HALVES - 1))

    def finish(k, h, r):
        queries, part, _ = tile(k, h, r)
        b_copy(k, h, r).wait_recv()
        out_ref[queries, part] += recv_b[queries, part].astype(jnp.float32)

    def a_sent(k, h, r):
        a_copy(k, h, r).wait_send()

    def b_sent(k, h, r):
        b_copy(k, h, r).wait_send()

    for k in range(4):
        s, xi, ci = place(k)
        parts = range(HALVES if k == 3 else 1)

        @pl.when(s == i)
        def _():
            for h in parts:
                each(k, (finish, h))

        @pl.when(ci != c)
        def _():
            for h in parts:
                each(k, (a_sent, h))

        @pl.when(s == other_x)
        def _():
            for h in parts:
                each(k, (b_sent, h))

    for h in range(HALVES):
        z_copy(z, order[1], 0, h).wait_send()
        for k in (1, 2, 3):
            y_copy(k, y, h).wait_send()

        @pl.when(mid)
        def _():
            z_copy(z, order[2], 1, h).wait_send()
            for k in (1, 2, 3):
                z_copy(order[k], onward[k], 1 + k, h).wait_send()


def fused(row_grads, query_grads, fisher_inv):
    layers, total, depth = row_grads.shape
    queries = query_grads.shape[1]
    bf16 = jnp.bfloat16
    dma = pltpu.SemaphoreType.DMA
    tiles = max(CHUNKS, HALVES * LAST_CHUNKS)
    out = pl.pallas_call(
        kernel,
        out_shape=jax.ShapeDtypeStruct((queries, total), jnp.float32),
        in_specs=[pl.BlockSpec(memory_space=pltpu.HBM)] * 3,
        out_specs=pl.BlockSpec(memory_space=pltpu.VMEM),
        scratch_shapes=[
            pltpu.VMEM((layers, total, depth), bf16),
            pltpu.VMEM((layers, queries, depth), bf16),
            pltpu.VMEM((layers, depth, depth), bf16),
            pltpu.VMEM((4, layers, queries, depth), bf16),
            pltpu.VMEM((3, queries, total), jnp.float32),
            pltpu.VMEM((2, queries, total), jnp.float32),
            pltpu.VMEM((2, queries, total), bf16),
            pltpu.VMEM((2, queries, total), bf16),
            pltpu.VMEM((queries, total), bf16),
            pltpu.VMEM((queries, total), bf16),
            dma((3,)), dma((CHUNKS,)),
            dma((5, HALVES)), dma((4, HALVES)), dma((4, HALVES)), dma((4, HALVES)),
            dma((2, tiles)), dma((2, tiles)), dma((tiles,)), dma((tiles,)),
        ],
        compiler_params=pltpu.CompilerParams(
            collective_id=0, has_side_effects=True, vmem_limit_bytes=50 * 2**20
        ),
    )(row_grads, query_grads, fisher_inv)
    return out.T


def solution(mesh):
    in_specs = (P("layer", ("grp", "ex"), None), P("layer", "ex", None), P("layer", None, None))
    out_specs = P(("grp", "ex"), "layer")

    def run(row_grads, query_grads, fisher_inv):
        two_layers = row_grads.shape[0] == 8
        small = (mesh.shape["grp"], mesh.shape["ex"], mesh.shape["layer"]) == (2, 4, 4)
        local = fused if small and two_layers else plain
        return jax.shard_map(
            local, mesh=mesh, in_specs=in_specs, out_specs=out_specs, check_vma=False
        )(row_grads, query_grads, fisher_inv)

    return run
```
